32 devices in a mesh: grp: 2 (over x), ex: 16 (over z, y, core).
Axes of the slice: x: 2, y: 2, z: 4, core: 2. Of those that a mesh axis runs over, the one named last changes fastest.
Arguments:
- values_store: bfloat16 [15360, 3, 2048], P('ex'), may hold values from -7.5 to 7.5, as said below
- scale_exps: int32 [15360, 3, 16], P('ex'), may hold values from -2 to 2
- test_grads: bfloat16 [3, 2048, 512], P(None, 'ex', 'grp'), parts along dimension 2, may hold values from -64 to 64
- lr_weights: float32 [3], replicated, may hold values from 0.3 to 3
- example_weights: float32 [15360], P('ex'), may hold values from 1 to 31
Outputs:
- influence: float32 [15360, 512], P('ex', 'grp'), parts along dimension 1
The draws below stay inside these ranges and needn't reach their ends.
There are 2 independent parts, one for each index of `grp`. The reference program is written for one: setup_inputs(seed, part) draws one part's arguments, and reference() takes and returns one part's arrays. A program takes and returns all parts, laid end to end along the dimension named above; an argument that names none is the same for every part. Nothing has to cross between parts.
Inputs may be any that keep to these rules, and one draw needn't show every extreme that they name: `values_store`: each value is s (8 + m) / 8 times 2 ** e with s = 1 or -1, m an integer 0 to 7 and e an integer -3 to 2.
All inputs are finite; a program needn't handle non-finite values.
Results may differ from the reference program's by a relative error of at most 0.0003.
Values may be sent and summed in bfloat16 or wider, within the bound.
A program may use at most 128 MiB of HBM per device.

```python
import math
import jax
import jax.numpy as jnp
from jax import lax

LAYERS = 4
DIMS = 512
BLOCK = 128
CKPTS = 3
QUERIES = 256
TRAIN_DEV = 960
NTRAIN = 15360


def draw_values_store(key, part):
    key = jax.random.fold_in(key, 11)
    key_sign, key_mant, key_expo = jax.random.split(key, 3)
    shape = (NTRAIN, CKPTS, LAYERS * DIMS)
    signs = jax.random.randint(key_sign, shape, 0, 2)
    mantissa = jax.random.randint(key_mant, shape, 0, 8)
    exponent = jax.random.randint(key_expo, shape, -3, 3)
    values = (1.0 - 2.0 * signs.astype(jnp.float32)) * (8.0 + mantissa.astype(jnp.float32)) / 8.0
    values = values * jnp.exp2(exponent.astype(jnp.float32))
    return values.astype(jnp.bfloat16)


def draw_test_grads(key, part):
    key = jax.random.fold_in(key, 23)
    key_scale, key_base = jax.random.split(key, 2)
    shape = (CKPTS, LAYERS * DIMS, QUERIES)
    spread = jnp.exp(math.log(10.0) * jax.random.uniform(key_scale, (CKPTS, 1, QUERIES)))
    values = jnp.clip(jax.random.normal(key_base, shape), -6.0, 6.0) * spread
    return values.astype(jnp.bfloat16)


def draw_example_weights(key, part):
    key = jax.random.fold_in(key, 37)
    rough = jnp.exp(math.log(10.0) * jax.random.uniform(key, (NTRAIN,)))
    position = jnp.arange(NTRAIN).astype(jnp.float32) / NTRAIN
    trend = jnp.exp(0.55 * position)
    return (rough * trend).astype(jnp.float32)


def touch_ends(entries, own_key, least, high):
    dims = entries.shape
    index_at = [jax.random.randint(jax.random.fold_in(own_key, axis), (), 0, dims[axis]) for axis in range(len(dims))]
    entries = entries.at[tuple(index_at)].set(least)
    longest = dims.index(max(dims))
    index_at[longest] = (index_at[longest] + 1) % dims[longest]
    return entries.at[tuple(index_at)].set(high)


def setup_inputs(seed: int = 0, part: int = 0) -> dict:
    seeds = jax.random.split(jax.random.key(seed), 6)
    own_keys = jax.random.split(jax.random.fold_in(seeds[5], part), 6)
    values_store = draw_values_store(jax.random.fold_in(seeds[5], 71), part)
    scale_exps = touch_ends(jax.random.randint(seeds[1], (NTRAIN, CKPTS, LAYERS * DIMS // BLOCK), -2, 3), jax.random.fold_in(seeds[1], 1), -2, 2).astype(jnp.int32)
    test_grads = draw_test_grads(jax.random.fold_in(jax.random.fold_in(seeds[5], part), 71), part)
    lr_weights = jnp.clip(jnp.exp(jax.random.uniform(seeds[3], (CKPTS,), jnp.float32, math.log(0.3), math.log(3.0))), 0.3, 3.0)
    example_weights = draw_example_weights(jax.random.fold_in(seeds[5], 71), part)
    return {"values_store": values_store, "scale_exps": scale_exps, "test_grads": test_grads, "lr_weights": lr_weights, "example_weights": example_weights}


EPSILON = 1e-06

def dequantize(values_store, scale_exps):
    factor = jnp.exp2(scale_exps.astype(jnp.float32)).astype(jnp.bfloat16)
    shaped = values_store.reshape(values_store.shape[:-1] + (scale_exps.shape[-1], -1))
    return (shaped * factor[..., None]).reshape(values_store.shape)

def checkpoint_sum(train_vals, test_block, lr_weights):
    partial_value = lr_weights[0] * jnp.dot(train_vals[:, 0, :], test_block[0], preferred_element_type=jnp.float32)
    for ckpt_index in range(1, train_vals.shape[1]):
        partial_value = partial_value + lr_weights[ckpt_index] * jnp.dot(train_vals[:, ckpt_index, :], test_block[ckpt_index], preferred_element_type=jnp.float32)
    return partial_value

def reference(values_store, scale_exps, test_grads, lr_weights, example_weights):
    examples_all = values_store.shape[0]
    block_count = examples_all // TRAIN_DEV
    grouped_vals = values_store.reshape(block_count, TRAIN_DEV, CKPTS, -1)
    grouped_exps = scale_exps.reshape(block_count, TRAIN_DEV, CKPTS, -1)

    def one_block(pair):
        train_vals = dequantize(pair[0], pair[1])
        return checkpoint_sum(train_vals, test_grads, lr_weights)
    partial_value = lax.map(one_block, (grouped_vals, grouped_exps)).reshape(examples_all, -1)
    weighted = example_weights[:, None] * partial_value
    square_sums = lax.optimization_barrier(jnp.sum(weighted * weighted, axis=0))
    return weighted / jnp.sqrt(square_sums / examples_all + EPSILON)
```

```python
import functools

import jax
import jax.numpy as jnp
from jax import lax
from jax.experimental import pallas as pl
from jax.experimental.pallas import tpu as pltpu
from jax.sharding import PartitionSpec as P

EPSILON = 1e-06
MESH = pl.DeviceIdType.MESH


def both(*conds):
    conds = [c for c in conds if c is not True]
    if not conds:
        return True
    out = conds[0]
    for c in conds[1:]:
        out = jnp.logical_and(out, c)
    return out


def run_if(cond, fn):
    if cond is True:
        fn()
    else:
        pl.when(cond)(fn)


def kernel(n, lines, cols, tg_ref, exps_ref, vals_hbm, lr_ref, ew_ref, w_out, sums_out,
           vals, gat, acc, ftin, ft, ftb, onehot, sums,
           recv_sem, send_sem, own_sem, vals_sem, out_sem, sum_send, sum_recv):
    ckpts, shard, queries = tg_ref.shape
    _, rows, depth = vals.shape
    blocks = exps_ref.shape[1]
    pieces = recv_sem.shape[1]
    chunks = vals_sem.shape[1]
    crows = rows // chunks

    me = lax.axis_index("ex")
    core = lax.rem(me, 2)
    chip = lax.div(me, 2)
    b = lax.rem(chip, cols)
    a = lax.div(chip, cols)

    def index(a_at, b_at, c_at):
        return (a_at * cols + b_at) * 2 + c_at

    def vals_copy(c, i):
        at = pl.ds(i * crows, crows)
        return pltpu.make_async_copy(vals_hbm.at[c, at], vals.at[c, at], vals_sem.at[c, i])

    def slot(ref, j, p):
        at = pl.ds(pl.multiple_of(j * shard, shard), shard)
        return ref.at[p, at] if pieces > 1 else ref.at[:, at]

    def own_piece(p):
        return tg_ref.at[p] if pieces > 1 else tg_ref

    own_copy = pltpu.make_async_copy(
        tg_ref, gat.at[:, pl.ds(pl.multiple_of(me * shard, shard), shard)], own_sem
    )
    own_copy.start()

    barrier = pltpu.get_barrier_semaphore()

    def greet(i, carry):
        peer = lax.rem(me + i, n)
        pl.semaphore_signal(barrier, inc=1, device_id={"ex": peer}, device_id_type=MESH)
        return carry

    lax.fori_loop(1, n, greet, 0, unroll=n <= 16)
    for c in range(ckpts):
        for i in range(chunks):
            vals_copy(c, i).start()

    a_steps = [(s, sign) for s in range(lines) for sign in ((0,) if s == 0 else (-1, 1))]
    if cols == 2:
        b_steps = [(0, 0), (1, None)]
    else:
        b_steps = [(t, sign) for t in range(cols) for sign in ((0,) if t == 0 else (-1, 1))]

    def describe(s, sa, t, sb):
        valid = []
        a_at, b_at = a, b
        if s:
            a_at = a + sa * s
            valid.append(a_at >= 0 if sa < 0 else a_at < lines)
        if t:
            if sb is None:
                b_at = 1 - b
            else:
                b_at = b + sb * t
                valid.append(b_at >= 0 if sb < 0 else b_at < cols)
        sends = []
        if t == 0:
            if s == 0 or sa < 0:
                sends.append((0, a + 1 < lines, index(a + 1, b, core)))
            if s == 0 or sa > 0:
                sends.append((1, a >= 1, index(a - 1, b, core)))
            if cols == 2:
                sends.append((2, True, index(a, 1 - b, core)))
            else:
                sends.append((2, b + 1 < cols, index(a, b + 1, core)))
                sends.append((3, b >= 1, index(a, b - 1, core)))
        elif sb is not None:
            if sb < 0:
                sends.append((2, b + 1 < cols, index(a, b + 1, core)))
            else:
                sends.append((3, b >= 1, index(a, b - 1, core)))
        sends.append((4, True, index(a, b, 1 - core)))
        return both(*valid), a_at, b_at, sends

    groups = {}
    for s, sa in a_steps:
        for t, sb in b_steps:
            groups.setdefault(s + t, []).append((t == 0 and s == 0,) + describe(s, sa, t, sb))

    def copy_of(own, a_at, b_at, direction, target, p):
        j = index(a_at, b_at, core)
        return pltpu.make_async_remote_copy(
            src_ref=own_piece(p) if own else slot(gat, j, p),
            dst_ref=slot(gat, j, p),
            send_sem=send_sem.at[direction, a_at * cols + b_at, p],
            recv_sem=recv_sem.at[j, p],
            device_id={"ex": target},
            device_id_type=MESH,
        )

    def arrived(j, p):
        return pltpu.make_async_copy(slot(gat, j, p), slot(gat, j, p), recv_sem.at[j, p])

    def forward(event, p):
        own, valid, a_at, b_at, sends = event

        def go():
            if not own:
                arrived(index(a_at, b_at, core), p).wait()
            for direction, cond, target in sends:
                run_if(cond, lambda d=direction, t=target: copy_of(own, a_at, b_at, d, t, p).start())

        run_if(valid, go)

    def settle(event, p):
        own, valid, a_at, b_at, sends = event

        def go():
            for direction, cond, target in sends:
                run_if(cond, lambda d=direction, t=target: copy_of(own, a_at, b_at, d, t, p).wait_send())

        run_if(valid, go)

    def partner_wait(event):
        _, valid, a_at, b_at, _ = event

        def go():
            for p in range(pieces):
                arrived(index(a_at, b_at, 1 - core), p).wait()

        run_if(valid, go)

    mrows = rows // 2 if rows % 32 == 0 else rows

    def product(k0, width):
        kat = pl.ds(k0, width)

        @pl.loop(0, rows // mrows)
        def _(i):
            at = pl.ds(pl.multiple_of(i * mrows, mrows), mrows)
            total = acc[at, :]
            for c in range(ckpts):
                total += lr_ref[c] * jnp.dot(
                    vals[c, at, kat], gat[c, kat, :], preferred_element_type=jnp.float32
                )
            acc[at, :] = total

    eager = (2 * shard) % 128 == 0

    def multiply(event):
        own, valid, a_at, b_at, _ = event

        def go():
            if own:
                own_copy.wait()
            partner_wait((own, True, a_at, b_at, None))
            k0 = (a_at * cols + b_at) * (2 * shard)
            product(pl.multiple_of(k0, 2 * shard), 2 * shard)

        run_if(valid, go)

    def dequantize(c, i):
        vals_copy(c, i).wait()
        sub = 48 if crows % 48 == 0 else 16

        @pl.loop(0, crows // sub)
        def _(k):
            at = pl.ds(pl.multiple_of(i * crows + k * sub, 16), sub)
            factor = jnp.dot(ftb[at, :], onehot[c], preferred_element_type=jnp.float32)
            vals[c, at, :] = vals[c, at, :] * factor.astype(jnp.bfloat16)

    pl.semaphore_wait(barrier, n - 1)
    for p in range(pieces):
        forward(groups[0][0], p)

    ftin[...] = jnp.zeros_like(ftin)
    for c in range(ckpts):
        power = jnp.left_shift(1, exps_ref[c] + 2).astype(jnp.float32) * 0.25
        ftin[c * blocks : (c + 1) * blocks, :rows] = power
    ew_at = ckpts * blocks
    ftin[ew_at : ew_at + 1, :rows] = ew_ref[...]
    for i in range(ftin.shape[1] // 128):
        turned = ftin[:, i * 128 : (i + 1) * 128].T
        ft[i * 128 : (i + 1) * 128, :] = turned
        ftb[i * 128 : (i + 1) * 128, :] = turned.astype(jnp.bfloat16)
    for c in range(ckpts):
        row = lax.broadcasted_iota(jnp.int32, onehot.shape[1:], 0)
        col = lax.broadcasted_iota(jnp.int32, onehot.shape[1:], 1)
        block = depth // blocks
        hit = (col >= (row - c * blocks) * block) & (col < (row - c * blocks + 1) * block)
        hit = hit & (row >= c * blocks) & (row < (c + 1) * blocks)
        onehot[c] = jnp.where(hit, 1.0, 0.0).astype(jnp.bfloat16)
    acc[...] = jnp.zeros_like(acc)

    units = [functools.partial(dequantize, c, i) for c in range(ckpts) for i in range(chunks)]
    for _ in range(chunks // 2):
        units.pop(0)()
    last = max(groups)
    for g in range(1, last + 1):
        for p in range(pieces):
            for event in groups[g]:
                forward(event, p)
            if g == 1:
                for _ in range(min(len(units), chunks)):
                    units.pop(0)()
        if g == 1:
            while units:
                units.pop(0)()
        if eager and g < last:
            for event in groups[g - 1]:
                multiply(event)
            if g == last - 1:
                for event in groups[g]:
                    multiply(event)
    if eager:
        for event in groups[last]:
            multiply(event)
    else:
        own_copy.wait()
        for g in range(last + 1):
            for event in groups[g]:
                partner_wait(event)
        width = 256 if depth % 256 == 0 else depth

        @pl.loop(0, depth // width)
        def _(i):
            product(pl.multiple_of(i * width, width), width)

    wrows = 48 if rows % 48 == 0 else 8

    def weigh(i, squares):
        at = pl.ds(pl.multiple_of(i * wrows, wrows), wrows)
        value = acc[at, :] * ft[at, ew_at : ew_at + 1]
        acc[at, :] = value
        return squares + jnp.sum((value * value).reshape(wrows // 8, 8, queries), axis=0)

    sums[me] = lax.fori_loop(0, rows // wrows, weigh, jnp.zeros((8, queries), jnp.float32))

    def sum_copy(peer):
        return pltpu.make_async_remote_copy(
            src_ref=sums.at[me], dst_ref=sums.at[me], send_sem=sum_send.at[peer],
            recv_sem=sum_recv.at[me], device_id={"ex": peer}, device_id_type=MESH,
        )

    def push(i, carry):
        sum_copy(lax.rem(me + i, n)).start()
        return carry

    def take(i, carry):
        source = lax.rem(me + i, n)
        pltpu.make_async_copy(sums.at[source], sums.at[source], sum_recv.at[source]).wait()
        return carry

    def sent(i, carry):
        sum_copy(lax.rem(me + i, n)).wait_send()
        return carry

    lax.fori_loop(1, n, push, 0, unroll=n <= 16)
    out_copy = pltpu.make_async_copy(acc, w_out, out_sem)
    out_copy.start()
    for g in range(last + 1):
        for event in groups[g]:
            for p in range(pieces):
                settle(event, p)
    lax.fori_loop(1, n, sent, 0, unroll=n <= 16)
    lax.fori_loop(1, n, take, 0, unroll=n <= 16)
    total = jnp.sum(sums[...], axis=0)
    sums_out[...] = jnp.sum(total, axis=0, keepdims=True)
    out_copy.wait()


def on_device(n, values_store, scale_exps, test_grads, lr_weights, example_weights):
    rows, ckpts, depth = values_store.shape
    blocks = scale_exps.shape[2]
    _, shard, queries = test_grads.shape
    chips = n // 2
    cols = 1
    while (2 * cols) ** 2 <= chips:
        cols *= 2
    lines = chips // cols
    pieces = ckpts if n <= 32 else 1
    chunks = 4 if rows % 64 == 0 else 1
    padded = -(-rows // 128) * 128
    vmem = pl.BlockSpec(memory_space=pltpu.VMEM)
    hbm = pl.BlockSpec(memory_space=pl.ANY)
    weighted, square_sums = pl.pallas_call(
        functools.partial(kernel, n, lines, cols),
        out_shape=(
            jax.ShapeDtypeStruct((rows, queries), jnp.float32),
            jax.ShapeDtypeStruct((1, queries), jnp.float32),
        ),
        in_specs=[hbm, vmem, hbm, pl.BlockSpec(memory_space=pltpu.SMEM), vmem],
        out_specs=(hbm, vmem),
        scratch_shapes=[
            pltpu.VMEM((ckpts, rows, depth), jnp.bfloat16),
            pltpu.VMEM((ckpts, n * shard, queries), jnp.bfloat16),
            pltpu.VMEM((rows, queries), jnp.float32),
            pltpu.VMEM((128, padded), jnp.float32),
            pltpu.VMEM((padded, 128), jnp.float32),
            pltpu.VMEM((padded, 128), jnp.bfloat16),
            pltpu.VMEM((ckpts, 128, depth), jnp.bfloat16),
            pltpu.VMEM((n, 8, queries), jnp.float32),
            pltpu.SemaphoreType.DMA((n, pieces)),
            pltpu.SemaphoreType.DMA((5, chips, pieces)),
            pltpu.SemaphoreType.DMA,
            pltpu.SemaphoreType.DMA((ckpts, chunks)),
            pltpu.SemaphoreType.DMA,
            pltpu.SemaphoreType.DMA((n,)),
            pltpu.SemaphoreType.DMA((n,)),
        ],
        compiler_params=pltpu.CompilerParams(
            collective_id=0, has_side_effects=True, vmem_limit_bytes=48 * 1024 * 1024
        ),
    )(
        test_grads,
        jnp.transpose(scale_exps, (1, 2, 0)),
        jnp.transpose(values_store, (1, 0, 2)),
        lr_weights,
        example_weights[None, :],
    )
    return weighted / jnp.sqrt(square_sums / (rows * n) + EPSILON)


def solution(mesh):
    return jax.shard_map(
        functools.partial(on_device, mesh.shape["ex"]),
        mesh=mesh,
        in_specs=(P("ex", None, None), P("ex", None, None), P(None, "ex", "grp"), P(), P("ex")),
        out_specs=P("ex", "grp"),
        check_vma=False,
    )
```

```python
import functools

import jax
import jax.numpy as jnp
from jax import lax
from jax.experimental import pallas as pl
from jax.experimental.pallas import tpu as pltpu
from jax.sharding import PartitionSpec as P

EPSILON = 1e-06
MESH = pl.DeviceIdType.MESH


def both(*conds):
    conds = [c for c in conds if c is not True]
    if not conds:
        return True
    out = conds[0]
    for c in conds[1:]:
        out = jnp.logical_and(out, c)
    return out


def run_if(cond, fn):
    if cond is True:
        fn()
    elif cond is not False:
        pl.when(cond)(fn)


def kernel(n, lines, cols, tg_ref, exps_hbm, vals_hbm, lr_hbm, ew_hbm, w_out, sums_out,
           exps_ref, lr_ref, ew_ref, small_sem, vals, gat, acc, ftin, ft, sums,
           recv_sem, send_sem, own_sem, vals_sem, out_sem, sum_send, sum_recv):
    ckpts, shard, queries = tg_ref.shape
    _, parts, rows, width = vals.shape
    blocks = exps_ref.shape[1]
    depth = parts * width
    block = depth // blocks
    pieces = recv_sem.shape[1]
    chunks = vals_sem.shape[1]
    crows = rows // chunks

    me = lax.axis_index("ex")
    core = lax.rem(me, 2)
    chip = lax.div(me, 2)
    b = lax.rem(chip, cols)
    a = lax.div(chip, cols)

    def index(a_at, b_at, c_at):
        return (a_at * cols + b_at) * 2 + c_at

    def vals_copy(c, i):
        at = pl.ds(i * crows, crows)
        return [
            pltpu.make_async_copy(
                vals_hbm.at[c, at, k * width : (k + 1) * width], vals.at[c, k, at], vals_sem.at[c, i, k]
            )
            for k in range(parts)
        ]

    def slot(ref, j, p):
        at = pl.ds(pl.multiple_of(j * shard, shard), shard)
        return ref.at[p, at] if pieces > 1 else ref.at[:, at]

    def own_piece(p):
        return tg_ref.at[p] if pieces > 1 else tg_ref

    own_copy = pltpu.make_async_copy(
        tg_ref, gat.at[:, pl.ds(pl.multiple_of(me * shard, shard), shard)], own_sem
    )
    small = [
        pltpu.make_async_copy(exps_hbm, exps_ref, small_sem.at[0]),
        pltpu.make_async_copy(ew_hbm, ew_ref, small_sem.at[1]),
        pltpu.make_async_copy(lr_hbm, lr_ref, small_sem.at[2]),
    ]

    barrier = pltpu.get_barrier_semaphore()

    def greet(i, carry):
        peer = lax.rem(me + i, n)
        pl.semaphore_signal(barrier, inc=1, device_id={"ex": peer}, device_id_type=MESH)
        return carry

    lax.fori_loop(1, n, greet, 0, unroll=n <= 16)
    for copy in small:
        copy.start()
    own_copy.start()
    for c in range(ckpts):
        for i in range(chunks):
            for copy in vals_copy(c, i):
                copy.start()

    a_steps = [(s, sign) for s in range(lines) for sign in ((0,) if s == 0 else (-1, 1))]
    if cols == 2:
        b_steps = [(0, 0), (1, None)]
    else:
        b_steps = [(t, sign) for t in range(cols) for sign in ((0,) if t == 0 else (-1, 1))]

    def describe(s, sa, t, sb):
        valid = []
        a_at, b_at = a, b
        if s:
            a_at = a + sa * s
            valid.append(a_at >= 0 if sa < 0 else a_at < lines)
        if t:
            if sb is None:
                b_at = 1 - b
            else:
                b_at = b + sb * t
                valid.append(b_at >= 0 if sb < 0 else b_at < cols)
        sends = []
        if t == 0:
            if s == 0 or sa < 0:
                sends.append((0, a + 1 < lines, index(a + 1, b, core)))
            if s == 0 or sa > 0:
                sends.append((1, a >= 1, index(a - 1, b, core)))
            if cols == 2:
                sends.append((2, True if s == 0 else "rows first", index(a, 1 - b, core)))
            else:
                sends.append((2, b + 1 < cols, index(a, b + 1, core)))
                sends.append((3, b >= 1, index(a, b - 1, core)))
        elif sb is None:
            if s == 0 or sa < 0:
                sends.append((0, ("columns first", a + 1 < lines), index(a + 1, b, core)))
            if s == 0 or sa > 0:
                sends.append((1, ("columns first", a >= 1), index(a - 1, b, core)))
        else:
            if sb < 0:
                sends.append((2, b + 1 < cols, index(a, b + 1, core)))
            else:
                sends.append((3, b >= 1, index(a, b - 1, core)))
        sends.append((4, True, index(a, b, 1 - core)))
        return both(*valid), a_at, b_at, sends

    groups = {}
    for s, sa in a_steps:
        for t, sb in b_steps:
            groups.setdefault(s + t, []).append((t == 0 and s == 0,) + describe(s, sa, t, sb))

    def copy_of(own, a_at, b_at, direction, target, p):
        j = index(a_at, b_at, core)
        return pltpu.make_async_remote_copy(
            src_ref=own_piece(p) if own else slot(gat, j, p),
            dst_ref=slot(gat, j, p),
            send_sem=send_sem.at[direction, a_at * cols + b_at, p],
            recv_sem=recv_sem.at[j, p],
            device_id={"ex": target},
            device_id_type=MESH,
        )

    def choose(cond, p):
        if cond == "rows first":
            return core == 1 if p == pieces - 1 else True
        if isinstance(cond, tuple):
            return jnp.logical_and(cond[1], core == 0) if p == pieces - 1 else False
        return cond

    def arrived(j, p):
        return pltpu.make_async_copy(slot(gat, j, p), slot(gat, j, p), recv_sem.at[j, p])

    def forward(event, p):
        own, valid, a_at, b_at, sends = event

        def go():
            if not own:
                arrived(index(a_at, b_at, core), p).wait()
            for direction, cond, target in sends:
                run_if(choose(cond, p), lambda d=direction, t=target: copy_of(own, a_at, b_at, d, t, p).start())

        run_if(valid, go)

    def settle(event, p):
        own, valid, a_at, b_at, sends = event

        def go():
            for direction, cond, target in sends:
                run_if(choose(cond, p), lambda d=direction, t=target: copy_of(own, a_at, b_at, d, t, p).wait_send())

        run_if(valid, go)

    def partner_wait(event):
        _, valid, a_at, b_at, _ = event

        def go():
            for p in range(pieces):
                arrived(index(a_at, b_at, 1 - core), p).wait()

        run_if(valid, go)

    mrows = rows // 2 if rows % 32 == 0 else rows

    def product(part):
        kat = pl.ds(pl.multiple_of(part * width, width), width)

        @pl.loop(0, rows // mrows)
        def _(i):
            at = pl.ds(pl.multiple_of(i * mrows, mrows), mrows)
            total = acc[at, :]
            for c in range(ckpts):
                total += lr_ref[c] * jnp.dot(
                    vals[c, part, at, :], gat[c, kat, :], preferred_element_type=jnp.float32
                )
            acc[at, :] = total

    eager = 2 * shard == width

    def multiply(event):
        own, valid, a_at, b_at, _ = event

        def go():
            if own:
                own_copy.wait()
            partner_wait((own, True, a_at, b_at, None))
            product(a_at * cols + b_at)

        run_if(valid, go)

    def dequantize(c, i):
        for copy in vals_copy(c, i):
            copy.wait()
        at = pl.ds(i * crows, crows)
        for j in range(blocks):
            part, lane = divmod(j * block, width)
            factor = jnp.broadcast_to(ft[at, c * blocks + j : c * blocks + j + 1], (crows, block))
            kat = slice(lane, lane + block)
            vals[c, part, at, kat] = vals[c, part, at, kat] * factor.astype(jnp.bfloat16)

    pl.semaphore_wait(barrier, n - 1)
    for p in range(pieces):
        forward(groups[0][0], p)

    for copy in small:
        copy.wait()
    ftin[...] = jnp.zeros_like(ftin)
    for c in range(ckpts):
        power = jnp.left_shift(1, exps_ref[c] + 2).astype(jnp.float32) * 0.25
        ftin[c * blocks : (c + 1) * blocks, :rows] = power
    ew_at = ckpts * blocks
    ftin[ew_at : ew_at + 1, :rows] = ew_ref[...]
    for i in range(ftin.shape[1] // 128):
        ft[i * 128 : (i + 1) * 128, :] = ftin[:, i * 128 : (i + 1) * 128].T
    acc[...] = jnp.zeros_like(acc)

    units = [functools.partial(dequantize, c, i) for c in range(ckpts) for i in range(chunks)]
    for _ in range(chunks // 2):
        units.pop(0)()
    last = max(groups)
    for g in range(1, last + 1):
        for p in range(pieces):
            for event in groups[g]:
                forward(event, p)
            if g == 1:
                for _ in range(min(len(units), chunks)):
                    units.pop(0)()
        if g == 1:
            while units:
                units.pop(0)()
        if eager and g < last:
            for event in groups[g - 1]:
                multiply(event)
            if g == last - 1:
                for event in groups[g]:
                    multiply(event)
    if eager:
        for event in groups[last]:
            multiply(event)
    else:
        own_copy.wait()
        for g in range(last + 1):
            for event in groups[g]:
                partner_wait(event)
        pl.loop(0, parts)(product)

    squares = jnp.zeros((8, queries), jnp.float32)
    outs = []
    for i in range(chunks):
        at = slice(i * crows, (i + 1) * crows)
        value = acc[at, :] * ft[at, ew_at : ew_at + 1]
        acc[at, :] = value
        outs.append(pltpu.make_async_copy(acc.at[at], w_out.at[at], out_sem.at[i]))
        outs[-1].start()
        squares += jnp.sum((value * value).reshape(crows // 8, 8, queries), axis=0)
    sums[me] = jnp.sum(squares, axis=0, keepdims=True)

    def sum_copy(peer):
        return pltpu.make_async_remote_copy(
            src_ref=sums.at[me], dst_ref=sums.at[me], send_sem=sum_send.at[peer],
            recv_sem=sum_recv.at[me], device_id={"ex": peer}, device_id_type=MESH,
        )

    def push(i, carry):
        sum_copy(lax.rem(me + i, n)).start()
        return carry

    def take(i, carry):
        source = lax.rem(me + i, n)
        pltpu.make_async_copy(sums.at[source], sums.at[source], sum_recv.at[source]).wait()
        return carry

    def sent(i, carry):
        sum_copy(lax.rem(me + i, n)).wait_send()
        return carry

    lax.fori_loop(1, n, push, 0, unroll=n <= 16)
    for g in range(last + 1):
        for event in groups[g]:
            for p in range(pieces):
                settle(event, p)
    lax.fori_loop(1, n, sent, 0, unroll=n <= 16)
    lax.fori_loop(1, n, take, 0, unroll=n <= 16)
    sums_out[...] = jnp.sum(sums[...], axis=0)
    for copy in outs:
        copy.wait()


def on_device(n, values_store, scale_exps, test_grads, lr_weights, example_weights):
    rows, ckpts, depth = values_store.shape
    blocks = scale_exps.shape[2]
    _, shard, queries = test_grads.shape
    chips = n // 2
    cols = 1
    while (2 * cols) ** 2 <= chips:
        cols *= 2
    lines = chips // cols
    pieces = ckpts if n <= 32 else 1
    chunks = 4 if rows % 64 == 0 else 1
    parts = depth // 256 if depth % 256 == 0 else 1
    padded = -(-rows // 128) * 128
    vmem = pl.BlockSpec(memory_space=pltpu.VMEM)
    hbm = pl.BlockSpec(memory_space=pltpu.HBM)
    weighted, square_sums = pl.pallas_call(
        functools.partial(kernel, n, lines, cols),
        out_shape=(
            jax.ShapeDtypeStruct((rows, queries), jnp.float32),
            jax.ShapeDtypeStruct((1, queries), jnp.float32),
        ),
        in_specs=[hbm] * 5,
        out_specs=(pl.BlockSpec(memory_space=pl.ANY), vmem),
        scratch_shapes=[
            pltpu.VMEM((ckpts, blocks, rows), jnp.int32),
            pltpu.SMEM((ckpts,), jnp.float32),
            pltpu.VMEM((1, rows), jnp.float32),
            pltpu.SemaphoreType.DMA((3,)),
            pltpu.VMEM((ckpts, parts, rows, depth // parts), jnp.bfloat16),
            pltpu.VMEM((ckpts, n * shard, queries), jnp.bfloat16),
            pltpu.VMEM((rows, queries), jnp.float32),
            pltpu.VMEM((128, padded), jnp.float32),
            pltpu.VMEM((padded, 128), jnp.float32),
            pltpu.VMEM((n, 1, queries), jnp.float32),
            pltpu.SemaphoreType.DMA((n, pieces)),
            pltpu.SemaphoreType.DMA((5, chips, pieces)),
            pltpu.SemaphoreType.DMA,
            pltpu.SemaphoreType.DMA((ckpts, chunks, parts)),
            pltpu.SemaphoreType.DMA((chunks,)),
            pltpu.SemaphoreType.DMA((n,)),
            pltpu.SemaphoreType.DMA((n,)),
        ],
        compiler_params=pltpu.CompilerParams(
            collective_id=0, has_side_effects=True, vmem_limit_bytes=60 * 1024 * 1024
        ),
    )(
        test_grads,
        jnp.transpose(scale_exps, (1, 2, 0)),
        jnp.transpose(values_store, (1, 0, 2)),
        lr_weights,
        example_weights[None, :],
    )
    return weighted / jnp.sqrt(square_sums / (rows * n) + EPSILON)


def solution(mesh):
    return jax.shard_map(
        functools.partial(on_device, mesh.shape["ex"]),
        mesh=mesh,
        in_specs=(P("ex", None, None), P("ex", None, None), P(None, "ex", "grp"), P(), P("ex")),
        out_specs=P("ex", "grp"),
        check_vma=False,
    )
```

```python
import functools

import jax
import jax.numpy as jnp
from jax import lax
from jax.experimental import pallas as pl
from jax.experimental.pallas import tpu as pltpu
from jax.sharding import PartitionSpec as P

EPSILON = 1e-06
MESH = pl.DeviceIdType.MESH


def both(*conds):
    conds = [c for c in conds if c is not True]
    if not conds:
        return True
    out = conds[0]
    for c in conds[1:]:
        out = jnp.logical_and(out, c)
    return out


def run_if(cond, fn):
    if cond is True:
        fn()
    elif cond is not False:
        pl.when(cond)(fn)


def kernel(n, lines, cols, tg_ref, exps_hbm, vals_hbm, lr_hbm, ew_hbm, w_out, sums_out,
           exps_ref, lr_ref, ew_ref, small_sem, vals, gat, acc, ftin, ft, sums,
           recv_sem, send_sem, own_sem, vals_sem, out_sem, sum_send, sum_recv):
    ckpts, shard, queries = tg_ref.shape
    _, parts, rows, width = vals.shape
    blocks = exps_ref.shape[1]
    depth = parts * width
    block = depth // blocks
    pieces = recv_sem.shape[1]
    chunks = vals_sem.shape[1]
    crows = rows // chunks

    me = lax.axis_index("ex")
    core = lax.rem(me, 2)
    chip = lax.div(me, 2)
    b = lax.rem(chip, cols)
    a = lax.div(chip, cols)

    def index(a_at, b_at, c_at):
        return (a_at * cols + b_at) * 2 + c_at

    def vals_copy(c, i):
        at = pl.ds(i * crows, crows)
        return [
            pltpu.make_async_copy(
                vals_hbm.at[c, at, k * width : (k + 1) * width], vals.at[c, k, at], vals_sem.at[c, i, k]
            )
            for k in range(parts)
        ]

    def slot(ref, j, p):
        at = pl.ds(pl.multiple_of(j * shard, shard), shard)
        return ref.at[p, at] if pieces > 1 else ref.at[:, at]

    def own_piece(p):
        return tg_ref.at[p] if pieces > 1 else tg_ref

    own_copy = pltpu.make_async_copy(
        tg_ref, gat.at[:, pl.ds(pl.multiple_of(me * shard, shard), shard)], own_sem
    )
    small = [
        pltpu.make_async_copy(exps_hbm, exps_ref, small_sem.at[0]),
        pltpu.make_async_copy(ew_hbm, ew_ref, small_sem.at[1]),
        pltpu.make_async_copy(lr_hbm, lr_ref, small_sem.at[2]),
    ]

    barrier = pltpu.get_barrier_semaphore()

    def greet(i, carry):
        peer = lax.rem(me + i, n)
        pl.semaphore_signal(barrier, inc=1, device_id={"ex": peer}, device_id_type=MESH)
        return carry

    lax.fori_loop(1, n, greet, 0, unroll=n <= 16)
    for copy in small:
        copy.start()
    own_copy.start()
    for c in range(ckpts):
        for i in range(chunks):
            for copy in vals_copy(c, i):
                copy.start()

    a_steps = [(s, sign) for s in range(lines) for sign in ((0,) if s == 0 else (-1, 1))]
    if cols == 2:
        b_steps = [(0, 0), (1, None)]
    else:
        b_steps = [(t, sign) for t in range(cols) for sign in ((0,) if t == 0 else (-1, 1))]

    def describe(s, sa, t, sb):
        valid = []
        a_at, b_at = a, b
        if s:
            a_at = a + sa * s
            valid.append(a_at >= 0 if sa < 0 else a_at < lines)
        if t:
            if sb is None:
                b_at = 1 - b
            else:
                b_at = b + sb * t
                valid.append(b_at >= 0 if sb < 0 else b_at < cols)
        sends = []
        if t == 0:
            if s == 0 or sa < 0:
                sends.append((0, a + 1 < lines, index(a + 1, b, core)))
            if s == 0 or sa > 0:
                sends.append((1, a >= 1, index(a - 1, b, core)))
            if cols == 2:
                sends.append((2, True if s == 0 else "rows first", index(a, 1 - b, core)))
            else:
                sends.append((2, b + 1 < cols, index(a, b + 1, core)))
                sends.append((3, b >= 1, index(a, b - 1, core)))
        elif sb is None:
            if s == 0 or sa < 0:
                sends.append((0, ("columns first", a + 1 < lines), index(a + 1, b, core)))
            if s == 0 or sa > 0:
                sends.append((1, ("columns first", a >= 1), index(a - 1, b, core)))
        else:
            if sb < 0:
                sends.append((2, b + 1 < cols, index(a, b + 1, core)))
            else:
                sends.append((3, b >= 1, index(a, b - 1, core)))
        sends.append((4, True, index(a, b, 1 - core)))
        return both(*valid), a_at, b_at, sends

    groups = {}
    for s, sa in a_steps:
        for t, sb in b_steps:
            groups.setdefault(2 * s + 3 * t, []).append((t == 0 and s == 0,) + describe(s, sa, t, sb))
    groups = [groups[key] for key in sorted(groups)]

    def copy_of(own, a_at, b_at, direction, target, p):
        j = index(a_at, b_at, core)
        return pltpu.make_async_remote_copy(
            src_ref=own_piece(p) if own else slot(gat, j, p),
            dst_ref=slot(gat, j, p),
            send_sem=send_sem.at[direction, a_at * cols + b_at, p],
            recv_sem=recv_sem.at[j, p],
            device_id={"ex": target},
            device_id_type=MESH,
        )

    def choose(cond, p):
        if cond == "rows first":
            return core == 1 if p == pieces - 1 else True
        if isinstance(cond, tuple):
            return jnp.logical_and(cond[1], core == 0) if p == pieces - 1 else False
        return cond

    def arrived(j, p):
        return pltpu.make_async_copy(slot(gat, j, p), slot(gat, j, p), recv_sem.at[j, p])

    def forward(event, p):
        own, valid, a_at, b_at, sends = event

        def go():
            if not own:
                arrived(index(a_at, b_at, core), p).wait()
            for direction, cond, target in sends:
                run_if(choose(cond, p), lambda d=direction, t=target: copy_of(own, a_at, b_at, d, t, p).start())

        run_if(valid, go)

    def settle(event, p):
        own, valid, a_at, b_at, sends = event

        def go():
            for direction, cond, target in sends:
                run_if(choose(cond, p), lambda d=direction, t=target: copy_of(own, a_at, b_at, d, t, p).wait_send())

        run_if(valid, go)

    def partner_wait(event):
        _, valid, a_at, b_at, _ = event

        def go():
            for p in range(pieces):
                arrived(index(a_at, b_at, 1 - core), p).wait()

        run_if(valid, go)

    mrows = rows // 2 if rows % 32 == 0 else rows

    def product(part):
        kat = pl.ds(pl.multiple_of(part * width, width), width)

        @pl.loop(0, rows // mrows)
        def _(i):
            at = pl.ds(pl.multiple_of(i * mrows, mrows), mrows)
            total = acc[at, :]
            for c in range(ckpts):
                total += lr_ref[c] * jnp.dot(
                    vals[c, part, at, :], gat[c, kat, :], preferred_element_type=jnp.float32
                )
            acc[at, :] = total

    eager = 2 * shard == width

    def multiply(event):
        own, valid, a_at, b_at, _ = event

        def go():
            if own:
                own_copy.wait()
            partner_wait((own, True, a_at, b_at, None))
            product(a_at * cols + b_at)

        run_if(valid, go)

    def dequantize(c, i):
        for copy in vals_copy(c, i):
            copy.wait()
        at = pl.ds(i * crows, crows)
        for j in range(blocks):
            part, lane = divmod(j * block, width)
            factor = jnp.broadcast_to(ft[at, c * blocks + j : c * blocks + j + 1], (crows, block))
            kat = slice(lane, lane + block)
            vals[c, part, at, kat] = vals[c, part, at, kat] * factor.astype(jnp.bfloat16)

    pl.semaphore_wait(barrier, n - 1)
    for p in range(pieces):
        forward(groups[0][0], p)

    for copy in small:
        copy.wait()
    ftin[...] = jnp.zeros_like(ftin)
    for c in range(ckpts):
        power = jnp.left_shift(1, exps_ref[c] + 2).astype(jnp.float32) * 0.25
        ftin[c * blocks : (c + 1) * blocks, :rows] = power
    ew_at = ckpts * blocks
    ftin[ew_at : ew_at + 1, :rows] = ew_ref[...]
    for i in range(ftin.shape[1] // 128):
        ft[i * 128 : (i + 1) * 128, :] = ftin[:, i * 128 : (i + 1) * 128].T
    acc[...] = jnp.zeros_like(acc)

    units = [functools.partial(dequantize, c, i) for c in range(ckpts) for i in range(chunks)]
    last = len(groups) - 1
    settled = 0
    for g in range(1, last + 1):
        if g == last:
            while settled < last - 2:
                for event in groups[settled]:
                    for p in range(pieces):
                        settle(event, p)
                settled += 1
        for p in range(pieces):
            for event in groups[g]:
                forward(event, p)
            for _ in range(2):
                if units:
                    units.pop(0)()
        if g >= 2:
            while units:
                units.pop(0)()
        if eager and 2 <= g < last:
            for event in groups[g - 2]:
                multiply(event)
            if g == last - 1:
                for event in groups[g - 1] + groups[g]:
                    multiply(event)
    while units:
        units.pop(0)()
    if eager:
        for event in groups[last]:
            multiply(event)
    else:
        own_copy.wait()
        for g in range(last + 1):
            for event in groups[g]:
                partner_wait(event)
        pl.loop(0, parts)(product)

    squares = jnp.zeros((8, queries), jnp.float32)
    outs = []
    for i in range(chunks):
        at = slice(i * crows, (i + 1) * crows)
        value = acc[at, :] * ft[at, ew_at : ew_at + 1]
        acc[at, :] = value
        outs.append(pltpu.make_async_copy(acc.at[at], w_out.at[at], out_sem.at[i]))
        outs[-1].start()
        squares += jnp.sum((value * value).reshape(crows // 8, 8, queries), axis=0)
    sums[me] = jnp.sum(squares, axis=0, keepdims=True)

    def sum_copy(peer):
        return pltpu.make_async_remote_copy(
            src_ref=sums.at[me], dst_ref=sums.at[me], send_sem=sum_send.at[peer],
            recv_sem=sum_recv.at[me], device_id={"ex": peer}, device_id_type=MESH,
        )

    def push(i, carry):
        sum_copy(lax.rem(me + i, n)).start()
        return carry

    def take(i, carry):
        source = lax.rem(me + i, n)
        pltpu.make_async_copy(sums.at[source], sums.at[source], sum_recv.at[source]).wait()
        return carry

    def sent(i, carry):
        sum_copy(lax.rem(me + i, n)).wait_send()
        return carry

    lax.fori_loop(1, n, push, 0, unroll=n <= 16)
    for g in range(settled, last + 1):
        for event in groups[g]:
            for p in range(pieces):
                settle(event, p)
    lax.fori_loop(1, n, sent, 0, unroll=n <= 16)
    lax.fori_loop(1, n, take, 0, unroll=n <= 16)
    sums_out[...] = jnp.sum(sums[...], axis=0)
    for copy in outs:
        copy.wait()


def on_device(n, values_store, scale_exps, test_grads, lr_weights, example_weights):
    rows, ckpts, depth = values_store.shape
    blocks = scale_exps.shape[2]
    _, shard, queries = test_grads.shape
    chips = n // 2
    cols = 1
    while (2 * cols) ** 2 <= chips:
        cols *= 2
    lines = chips // cols
    pieces = ckpts if n <= 32 else 1
    chunks = 4 if rows % 64 == 0 else 1
    parts = depth // 256 if depth % 256 == 0 else 1
    padded = -(-rows // 128) * 128
    vmem = pl.BlockSpec(memory_space=pltpu.VMEM)
    hbm = pl.BlockSpec(memory_space=pltpu.HBM)
    weighted, square_sums = pl.pallas_call(
        functools.partial(kernel, n, lines, cols),
        out_shape=(
            jax.ShapeDtypeStruct((rows, queries), jnp.float32),
            jax.ShapeDtypeStruct((1, queries), jnp.float32),
        ),
        in_specs=[hbm] * 5,
        out_specs=(pl.BlockSpec(memory_space=pl.ANY), vmem),
        scratch_shapes=[
            pltpu.VMEM((ckpts, blocks, rows), jnp.int32),
            pltpu.SMEM((ckpts,), jnp.float32),
            pltpu.VMEM((1, rows), jnp.float32),
            pltpu.SemaphoreType.DMA((3,)),
            pltpu.VMEM((ckpts, parts, rows, depth // parts), jnp.bfloat16),
            pltpu.VMEM((ckpts, n * shard, queries), jnp.bfloat16),
            pltpu.VMEM((rows, queries), jnp.float32),
            pltpu.VMEM((128, padded), jnp.float32),
            pltpu.VMEM((padded, 128), jnp.float32),
            pltpu.VMEM((n, 1, queries), jnp.float32),
            pltpu.SemaphoreType.DMA((n, pieces)),
            pltpu.SemaphoreType.DMA((5, chips, pieces)),
            pltpu.SemaphoreType.DMA,
            pltpu.SemaphoreType.DMA((ckpts, chunks, parts)),
            pltpu.SemaphoreType.DMA((chunks,)),
            pltpu.SemaphoreType.DMA((n,)),
            pltpu.SemaphoreType.DMA((n,)),
        ],
        compiler_params=pltpu.CompilerParams(
            collective_id=0, has_side_effects=True, vmem_limit_bytes=60 * 1024 * 1024
        ),
    )(
        test_grads,
        jnp.transpose(scale_exps, (1, 2, 0)),
        jnp.transpose(values_store, (1, 0, 2)),
        lr_weights,
        example_weights[None, :],
    )
    return weighted / jnp.sqrt(square_sums / (rows * n) + EPSILON)


def solution(mesh):
    return jax.shard_map(
        functools.partial(on_device, mesh.shape["ex"]),
        mesh=mesh,
        in_specs=(P("ex", None, None), P("ex", None, None), P(None, "ex", "grp"), P(), P("ex")),
        out_specs=P("ex", "grp"),
        check_vma=False,
    )
```
